32 devices in a mesh: groups: 2 (over x), ia: 16 (over z, y, core).
Axes of the slice: x: 2, y: 2, z: 4, core: 2. Of those that a mesh axis runs over, the one named last changes fastest.
Arguments:
- pair: bfloat16 [512, 256, 128], P(('groups', 'ia')), parts along dimension 0, may hold values from -6 to 6
- pad_mask: int32 [512], P('groups'), parts along dimension 0, may hold values 0 or 1
- w_in: bfloat16 [128, 640], replicated, may hold values from -0.5 to 0.5
- in_exps: int32 [20], replicated, may hold values from -1 to 1
- w_out: bfloat16 [128, 128], replicated, may hold values from -0.5 to 0.5
- out_exps: int32 [4], replicated, may hold values from -1 to 1, as said below
- in_gain: float32 [128], replicated, may hold values from 0.1 to 1.9
- in_bias: float32 [128], replicated, may hold values from -3 to 3
- out_gain: float32 [128], replicated, may hold values from 0.1 to 1.9
- out_bias: float32 [128], replicated, may hold values from -3 to 3
Outputs:
- update: bfloat16 [512, 256, 128], P(('groups', 'ia')), parts along dimension 0
The draws below stay inside these ranges and needn't reach their ends.
There are 2 independent parts, one for each index of `groups`. The reference program is written for one: setup_inputs(seed, part) draws one part's arguments, and reference() takes and returns one part's arrays. A program takes and returns all parts, laid end to end along the dimension named above; an argument that names none is the same for every part. Nothing has to cross between parts.
Inputs may be any that keep to these rules, and one draw needn't show every extreme that they name: `out_exps`: power-of-two exponents of the output projection's column blocks.
All inputs are finite; a program needn't handle non-finite values.
Results may differ from the reference program's by a relative error of at most 0.0085.
Values may be sent and summed in bfloat16 or wider, within the bound.
A program may use at most 128 MiB of HBM per device.

```python
import jax
import jax.numpy as jnp
from jax import lax

C = 128
H = 128
BLK = 32
TOKENS = 256


def draw_out_exps(key, part):
    key = jax.random.fold_in(key, 11)
    count = C // BLK
    start = jax.random.randint(key, (), 0, 3, dtype=jnp.int32)
    stride = jax.random.randint(jax.random.fold_in(key, 1), (), 1, 3, dtype=jnp.int32)
    places = jnp.arange(count, dtype=jnp.int32)
    return ((start + places * stride) % 3 - 1).astype(jnp.int32)


def place_ends(array, rng, least, largest):
    index_at = [jax.random.randint(jax.random.fold_in(rng, axis), (), 0, length) for axis, length in enumerate(array.shape)]
    widest = array.shape.index(max(array.shape))
    beside = index_at[:widest] + [(index_at[widest] + 1) % array.shape[widest]] + index_at[widest + 1:]
    return array.at[tuple(index_at)].set(least).at[tuple(beside)].set(largest)


def levels(rng, dims, pieces, smallest, top_value):
    level = 1.0
    for axis_at, parts in pieces:
        steps = jax.random.uniform(jax.random.fold_in(jax.random.fold_in(rng, 6), axis_at), (parts,), jnp.float32, smallest / len(pieces), top_value / len(pieces))
        level = level * jnp.repeat(jnp.exp(steps), dims[axis_at] // parts).reshape((-1,) + (1,) * (len(dims) - 1 - axis_at))
    return level


def bell_draw(key, dims, scale, bound, split=(), kind=jnp.bfloat16):
    values = scale * jax.random.normal(key, dims, jnp.float32)
    if split:
        values = values * levels(key, dims, split, -0.22, 0.18)
    return jnp.clip(values, -bound, bound).astype(kind)


def setup_inputs(seed: int = 0, part: int = 0) -> dict:
    arg_keys = jax.random.split(jax.random.key(seed), 11)
    part_splits = jax.random.split(jax.random.fold_in(arg_keys[10], part), 11)
    pair = bell_draw(part_splits[0], (TOKENS, TOKENS, C), 1.0, 6.0, ((0, 16),))
    pad_mask = place_ends((jax.random.randint(part_splits[1], (TOKENS,), 0, 8) < 7).astype(jnp.int32), jax.random.fold_in(part_splits[1], 1), 0, 1)
    w_in = bell_draw(arg_keys[2], (C, 5 * H), C ** -0.5, 0.5)
    in_exps = place_ends(jax.random.randint(arg_keys[3], (5 * H // BLK,), -1, 2), jax.random.fold_in(arg_keys[3], 1), -1, 1).astype(jnp.int32)
    w_out = bell_draw(arg_keys[4], (H, C), H ** -0.5, 0.5)
    out_exps = draw_out_exps(jax.random.fold_in(arg_keys[10], 71), part)
    in_gain = jnp.clip(1.0 + 0.18 * jax.random.normal(arg_keys[6], (C,), jnp.float32), 0.1, 1.9)
    in_bias = bell_draw(arg_keys[7], (C,), 0.5, 3.0, (), jnp.float32)
    out_gain = jnp.clip(1.0 + 0.18 * jax.random.normal(arg_keys[8], (H,), jnp.float32), 0.1, 1.9)
    out_bias = bell_draw(arg_keys[9], (H,), 0.5, 3.0, (), jnp.float32)
    return {"pair": pair, "pad_mask": pad_mask, "w_in": w_in, "in_exps": in_exps, "w_out": w_out, "out_exps": out_exps, "in_gain": in_gain, "in_bias": in_bias, "out_gain": out_gain, "out_bias": out_bias}


def layer_norm(values, gain, bias, axis):
    mean_val = lax.optimization_barrier(jnp.mean(values, axis=axis, keepdims=True))
    centred = values - mean_val
    variance = lax.optimization_barrier(jnp.mean(centred * centred, axis=axis, keepdims=True))
    return centred * lax.rsqrt(variance + 1e-05) * gain + bias

def scaled_weight(weight, exponents):
    factor = jnp.repeat(jnp.exp2(exponents.astype(jnp.float32)), BLK)
    return (weight.astype(jnp.float32) * factor[None, :]).astype(jnp.bfloat16)

def reference(pair, pad_mask, w_in, in_exps, w_out, out_exps, in_gain, in_bias, out_gain, out_bias):
    w_eff = scaled_weight(w_in, in_exps)
    w_last = scaled_weight(w_out, out_exps)
    mask_f = pad_mask.astype(jnp.float32)

    def project_row(row_index):
        row_vals = lax.dynamic_index_in_dim(pair, row_index, 0, keepdims=False).astype(jnp.float32)
        normed = layer_norm(row_vals, in_gain, in_bias, -1).astype(jnp.bfloat16)
        proj = jnp.dot(normed, w_eff, preferred_element_type=jnp.float32)
        pair_mask = mask_f[row_index] * mask_f[:, None]
        left = (jax.nn.sigmoid(proj[:, 0:H]) * proj[:, H:2 * H] * pair_mask).astype(jnp.bfloat16)
        right = (jax.nn.sigmoid(proj[:, 2 * H:3 * H]) * proj[:, 3 * H:4 * H] * pair_mask).astype(jnp.bfloat16)
        gate = jax.nn.sigmoid(proj[:, 4 * H:5 * H]).astype(jnp.bfloat16)
        return (left.T, right.T, gate)
    indices = jnp.arange(TOKENS, dtype=jnp.int32)
    left_t, right_t, gate = lax.map(project_row, indices)

    def channel_product(chan):
        left_h = lax.dynamic_index_in_dim(left_t, chan, 1, keepdims=False).astype(jnp.float32)
        right_h = lax.dynamic_index_in_dim(right_t, chan, 1, keepdims=False).astype(jnp.float32)
        return jnp.dot(left_h, right_h.T, precision=lax.Precision.HIGHEST).astype(jnp.bfloat16)
    tri = lax.map(channel_product, jnp.arange(H, dtype=jnp.int32))

    def finish_row(row_index):
        tri_row = lax.dynamic_index_in_dim(tri, row_index, 1, keepdims=False).astype(jnp.float32)
        tri_norm = layer_norm(tri_row, out_gain[:, None], out_bias[:, None], 0).astype(jnp.bfloat16)
        mixed = jnp.dot(tri_norm.T, w_last, preferred_element_type=jnp.float32)
        gate_row = lax.dynamic_index_in_dim(gate, row_index, 0, keepdims=False).astype(jnp.float32)
        return (mixed * gate_row).astype(jnp.bfloat16)
    rows_out = lax.map(finish_row, indices)
    return jnp.swapaxes(rows_out, 0, 1)
```

```python
import functools

import jax
import jax.numpy as jnp
from jax import lax
from jax.experimental import pallas as pl
from jax.experimental.pallas import tpu as pltpu
from jax.sharding import PartitionSpec as P

BLK = 32


def layer_norm(values, gain, bias, axis):
    mean_val = jnp.mean(values, axis=axis, keepdims=True)
    centred = values - mean_val
    variance = jnp.mean(centred * centred, axis=axis, keepdims=True)
    return centred * lax.rsqrt(variance + 1e-05) * gain + bias


def scaled_weight(weight, exponents):
    factor = jnp.repeat(jnp.exp2(exponents.astype(jnp.float32)), BLK)
    return (weight.astype(jnp.float32) * factor[None, :]).astype(jnp.bfloat16)


def shards(pair, pad_mask, w_in, in_exps, w_out, out_exps, in_gain, in_bias, out_gain, out_bias):
    tok_rows = pair.shape[0]
    whole_len = pair.shape[1]
    width_in = pair.shape[2]
    hidden = w_out.shape[0]
    row_start = lax.axis_index("ia") * tok_rows
    w_eff = scaled_weight(w_in, in_exps)
    w_last = scaled_weight(w_out, out_exps)
    mask_f = pad_mask.astype(jnp.float32)
    mask_rows = lax.dynamic_slice_in_dim(mask_f, row_start, tok_rows, 0)
    normed = layer_norm(pair.astype(jnp.float32), in_gain, in_bias, -1).astype(jnp.bfloat16)
    proj = jnp.dot(
        normed.reshape(tok_rows * whole_len, width_in), w_eff, preferred_element_type=jnp.float32
    )
    proj = proj.reshape(tok_rows, whole_len, 5 * hidden)
    pair_mask = mask_rows[:, None, None] * mask_f[None, :, None]
    left = (
        jax.nn.sigmoid(proj[:, :, 0:hidden]) * proj[:, :, hidden : 2 * hidden] * pair_mask
    ).astype(jnp.bfloat16)
    right = (
        jax.nn.sigmoid(proj[:, :, 2 * hidden : 3 * hidden])
        * proj[:, :, 3 * hidden : 4 * hidden]
        * pair_mask
    ).astype(jnp.bfloat16)
    gate = jax.nn.sigmoid(proj[:, :, 4 * hidden : 5 * hidden]).astype(jnp.bfloat16)
    left_t = jnp.transpose(left, (2, 0, 1))
    right_t = jnp.transpose(right, (2, 0, 1))
    left_chan, right_chan = (
        lax.all_to_all(left_t, "ia", split_axis=0, concat_axis=1, tiled=True),
        lax.all_to_all(right_t, "ia", split_axis=0, concat_axis=1, tiled=True),
    )
    gate_moved = lax.all_to_all(gate, "ia", split_axis=1, concat_axis=0, tiled=True)
    gate_cols = jnp.swapaxes(gate_moved, 0, 1)
    tri_t = jnp.einsum(
        "hjk,hik->hji", right_chan, left_chan, preferred_element_type=jnp.float32
    ).astype(jnp.bfloat16)
    tri_cols = lax.all_to_all(tri_t, "ia", split_axis=1, concat_axis=0, tiled=True)
    tri_norm = layer_norm(
        tri_cols.astype(jnp.float32), out_gain[:, None, None], out_bias[:, None, None], 0
    ).astype(jnp.bfloat16)
    mixed = jnp.einsum("hji,hc->jic", tri_norm, w_last, preferred_element_type=jnp.float32)
    return (mixed * gate_cols.astype(jnp.float32)).astype(jnp.bfloat16)


CORE, Y, Z, HALF = 1, 2, 4, 8
CHIPS = (0, Z, Y, Z | Y)


def gated(normed, weight, mask):
    hidden = weight.shape[1] // 2
    rows, cols, width = normed.shape
    proj = jnp.dot(normed.reshape(rows * cols, width), weight, preferred_element_type=jnp.float32)
    proj = proj.reshape(rows, cols, 2 * hidden)
    value = (jax.nn.sigmoid(proj[:, :, :hidden]) * proj[:, :, hidden:] * mask).astype(jnp.bfloat16)
    return jnp.transpose(value, (2, 0, 1))


def place(rows, *refs):
    me = lax.axis_index("ia")
    out_ref = refs[-1]
    at = 0
    for far in (0, HALF):
        for chip in CHIPS:
            for core in (0, CORE):
                start = pl.multiple_of((me ^ (far | chip | core)) * rows, rows)
                out_ref[:, pl.ds(start, rows), :] = refs[at][:, core * rows : (core + 1) * rows, :]
            at += 1


def half_shards(
    count, pair, pad_mask, w_in, in_exps, w_out, out_exps, in_gain, in_bias, out_gain, out_bias
):
    rows, whole_len, _ = pair.shape
    hidden = w_out.shape[0]
    me = lax.axis_index("ia")

    def swap(array, bits):
        return lax.ppermute(array, "ia", [(at, at ^ bits) for at in range(count)])

    w_eff = scaled_weight(w_in, in_exps)
    w_last = scaled_weight(w_out, out_exps)
    mask_f = pad_mask.astype(jnp.float32)

    def pair_mask(owner):
        own = lax.dynamic_slice_in_dim(mask_f, owner * rows, rows, 0)
        return own[:, None, None] * mask_f[None, :, None]

    def norm_in(values):
        return layer_norm(values.astype(jnp.float32), in_gain, in_bias, -1).astype(jnp.bfloat16)

    def gates(normed):
        parts = [
            lax.dynamic_slice_in_dim(normed, (me ^ core ^ chip) * rows, rows, 1)
            for core in (0, CORE)
            for chip in CHIPS
        ]
        picked = jnp.concatenate(parts, 1)
        proj = jnp.dot(
            picked.reshape(-1, picked.shape[2]),
            w_eff[:, 4 * hidden :],
            preferred_element_type=jnp.float32,
        )
        gate = jax.nn.sigmoid(proj).astype(jnp.bfloat16).reshape(rows, 2, 4 * rows, hidden)
        return gate[:, 0], gate[:, 1]

    pair_far = swap(pair, HALF)
    normed = norm_in(pair)
    right = gated(normed, w_eff[:, 2 * hidden : 4 * hidden], pair_mask(me))
    right_z = swap(right, Z)
    right_y = swap(right, Y)
    right_zy = swap(right_z, Y)
    rights = jnp.concatenate([right, right_z, right_y, right_zy], 1)

    def finish(normed_rows, owner):
        left = gated(normed_rows, w_eff[:, : 2 * hidden], pair_mask(owner))
        gate_mine, gate_other = gates(normed_rows)
        lefts = jnp.concatenate([left, swap(left, CORE)], 1)
        gate = jnp.concatenate([gate_mine, swap(gate_other, CORE)], 0)
        tri = jnp.einsum(
            "hjk,hik->hji", rights, lefts, preferred_element_type=jnp.float32
        ).astype(jnp.bfloat16)
        tri_norm = layer_norm(
            tri.astype(jnp.float32), out_gain[:, None, None], out_bias[:, None, None], 0
        ).astype(jnp.bfloat16)
        mixed = jnp.einsum("hji,hc->jic", tri_norm, w_last, preferred_element_type=jnp.float32)
        update = (mixed * jnp.swapaxes(gate, 0, 1).astype(jnp.float32)).astype(jnp.bfloat16)
        blocks = [update[at * rows : (at + 1) * rows] for at in range(4)]
        return [blocks[0]] + [swap(block, chip) for block, chip in zip(blocks[1:], CHIPS[1:])]

    pieces = finish(normed, me) + finish(norm_in(pair_far), me ^ HALF)
    return pl.pallas_call(
        functools.partial(place, rows),
        out_shape=jax.ShapeDtypeStruct(pair.shape, jnp.bfloat16),
        in_specs=[pl.BlockSpec(memory_space=pltpu.VMEM)] * len(pieces),
        out_specs=pl.BlockSpec(memory_space=pltpu.VMEM),
    )(*pieces)


def solution(mesh):
    count = mesh.shape["ia"]
    body = functools.partial(half_shards, count) if count == 16 else shards
    return jax.shard_map(
        body,
        mesh=mesh,
        in_specs=(
            P(("groups", "ia"), None, None),
            P("groups"),
            P(),
            P(),
            P(),
            P(),
            P(),
            P(),
            P(),
            P(),
        ),
        out_specs=P(("groups", "ia"), None, None),
        check_vma=False,
    )
```

```python
import functools

import jax
import jax.numpy as jnp
from jax import lax
from jax.experimental import pallas as pl
from jax.experimental.pallas import tpu as pltpu
from jax.sharding import PartitionSpec as P

BLK = 32


def layer_norm(values, gain, bias, axis):
    mean_val = jnp.mean(values, axis=axis, keepdims=True)
    centred = values - mean_val
    variance = jnp.mean(centred * centred, axis=axis, keepdims=True)
    return centred * lax.rsqrt(variance + 1e-05) * gain + bias


def scaled_weight(weight, exponents):
    factor = jnp.repeat(jnp.exp2(exponents.astype(jnp.float32)), BLK)
    return (weight.astype(jnp.float32) * factor[None, :]).astype(jnp.bfloat16)


def shards(pair, pad_mask, w_in, in_exps, w_out, out_exps, in_gain, in_bias, out_gain, out_bias):
    tok_rows = pair.shape[0]
    whole_len = pair.shape[1]
    width_in = pair.shape[2]
    hidden = w_out.shape[0]
    row_start = lax.axis_index("ia") * tok_rows
    w_eff = scaled_weight(w_in, in_exps)
    w_last = scaled_weight(w_out, out_exps)
    mask_f = pad_mask.astype(jnp.float32)
    mask_rows = lax.dynamic_slice_in_dim(mask_f, row_start, tok_rows, 0)
    normed = layer_norm(pair.astype(jnp.float32), in_gain, in_bias, -1).astype(jnp.bfloat16)
    proj = jnp.dot(
        normed.reshape(tok_rows * whole_len, width_in), w_eff, preferred_element_type=jnp.float32
    )
    proj = proj.reshape(tok_rows, whole_len, 5 * hidden)
    pair_mask = mask_rows[:, None, None] * mask_f[None, :, None]
    left = (
        jax.nn.sigmoid(proj[:, :, 0:hidden]) * proj[:, :, hidden : 2 * hidden] * pair_mask
    ).astype(jnp.bfloat16)
    right = (
        jax.nn.sigmoid(proj[:, :, 2 * hidden : 3 * hidden])
        * proj[:, :, 3 * hidden : 4 * hidden]
        * pair_mask
    ).astype(jnp.bfloat16)
    gate = jax.nn.sigmoid(proj[:, :, 4 * hidden : 5 * hidden]).astype(jnp.bfloat16)
    left_t = jnp.transpose(left, (2, 0, 1))
    right_t = jnp.transpose(right, (2, 0, 1))
    left_chan, right_chan = (
        lax.all_to_all(left_t, "ia", split_axis=0, concat_axis=1, tiled=True),
        lax.all_to_all(right_t, "ia", split_axis=0, concat_axis=1, tiled=True),
    )
    gate_moved = lax.all_to_all(gate, "ia", split_axis=1, concat_axis=0, tiled=True)
    gate_cols = jnp.swapaxes(gate_moved, 0, 1)
    tri_t = jnp.einsum(
        "hjk,hik->hji", right_chan, left_chan, preferred_element_type=jnp.float32
    ).astype(jnp.bfloat16)
    tri_cols = lax.all_to_all(tri_t, "ia", split_axis=1, concat_axis=0, tiled=True)
    tri_norm = layer_norm(
        tri_cols.astype(jnp.float32), out_gain[:, None, None], out_bias[:, None, None], 0
    ).astype(jnp.bfloat16)
    mixed = jnp.einsum("hji,hc->jic", tri_norm, w_last, preferred_element_type=jnp.float32)
    return (mixed * gate_cols.astype(jnp.float32)).astype(jnp.bfloat16)


CORE, Y, Z, HALF = 1, 2, 4, 8
CHIPS = (0, Z, Y, Z | Y)
FAR_CHUNKS = 4
RIGHT_CHUNKS = 4


def other(me, bits):
    for bit in (CORE, Y, Z, HALF):
        if bits & bit:
            me = me + bit * (1 - 2 * ((me // bit) % 2))
    return me


def sigmoid(values):
    return 0.5 + 0.5 * jnp.tanh(0.5 * values)


def triangle(
    rows,
    whole_len,
    hidden,
    pair_ref,
    mask_ref,
    side_w_ref,
    gate_w_ref,
    last_w_ref,
    in_gain_ref,
    in_bias_ref,
    out_gain_ref,
    out_bias_ref,
    out_ref,
    far_ref,
    norm_ref,
    stage_ref,
    gate_stage_ref,
    right_ref,
    left_ref,
    gate_ref,
    gate_send_ref,
    tri_ref,
    update_ref,
    send_sem,
    recv_sem,
):
    me = lax.axis_index("ia")
    barrier = pltpu.get_barrier_semaphore()
    peers = (CORE, Y, Z, Z | Y, HALF)
    for bits in peers:
        pl.semaphore_signal(
            barrier, inc=1, device_id={"ia": other(me, bits)}, device_id_type=pl.DeviceIdType.MESH
        )
    pl.semaphore_wait(barrier, len(peers))

    started = []

    def send(src, dst, bits):
        at = len(started)
        copy = pltpu.make_async_remote_copy(
            src_ref=src,
            dst_ref=dst,
            send_sem=send_sem.at[at],
            recv_sem=recv_sem.at[at],
            device_id={"ia": other(me, bits)},
            device_id_type=pl.DeviceIdType.MESH,
        )
        copy.start()
        started.append(copy)
        return copy

    far_rows = rows // FAR_CHUNKS
    far_copies = []
    for at in range(FAR_CHUNKS):
        part = pl.ds(at * far_rows, far_rows)
        far_copies.append(send(pair_ref.at[part], far_ref.at[part], HALF))

    contract_last = (((1,), (1,)), ((), ()))
    contract_first = (((0,), (0,)), ((), ()))

    def normalise(src_ref, row):
        values = src_ref[row].astype(jnp.float32)
        normed = layer_norm(values, in_gain_ref[...], in_bias_ref[...], -1)
        norm_ref[row] = normed.astype(jnp.bfloat16)

    def project(row, side, mask_row):
        weight = side_w_ref[side * 2 * hidden : (side + 1) * 2 * hidden, :]
        proj = lax.dot_general(
            weight, norm_ref[row], contract_last, preferred_element_type=jnp.float32
        )
        value = sigmoid(proj[:hidden]) * proj[hidden:] * mask_ref[mask_row]
        for lane in range(whole_len // 128):
            stage_ref[lane, pl.ds(row, hidden, stride=rows), :] = value[
                :, lane * 128 : (lane + 1) * 128
            ]

    def unstage(dst_ref, slot, start, size):
        for lane in range(whole_len // 128):
            dst_ref[slot, start : start + size, :, lane * 128 : (lane + 1) * 128] = (
                stage_ref[lane, start * rows : (start + size) * rows, :]
                .reshape(size, rows, 128)
                .astype(jnp.bfloat16)
            )

    @pl.loop(0, rows)
    def _(row):
        normalise(pair_ref, row)
        project(row, 1, row)

    part_size = hidden // RIGHT_CHUNKS
    z_copies, y_copies = [], []
    for at in range(RIGHT_CHUNKS):
        unstage(right_ref, 0, at * part_size, part_size)
        part = pl.ds(at * part_size, part_size)
        z_copies.append(send(right_ref.at[0, part], right_ref.at[1, part], Z))
        y_copies.append(send(right_ref.at[0, part], right_ref.at[2, part], Y))

    gate_cols = [
        pl.ds(pl.multiple_of(other(me, core | chip) * rows, rows), rows)
        for core in (0, CORE)
        for chip in CHIPS
    ]
    cols = rows * len(CHIPS)

    def gates(row):
        picked = jnp.concatenate([norm_ref[row, part, :] for part in gate_cols], 0)
        gate = sigmoid(jnp.dot(picked, gate_w_ref[...], preferred_element_type=jnp.float32))
        gate_stage_ref[pl.ds(row, 2 * cols, stride=rows), :] = gate

    def finish_rows(slot):
        unstage(left_ref, slot, 0, hidden)
        gate_ref[slot] = (
            gate_stage_ref[0 : cols * rows, :].reshape(cols, rows, hidden).astype(jnp.bfloat16)
        )
        gate_send_ref[slot // 2] = (
            gate_stage_ref[cols * rows :, :].reshape(cols, rows, hidden).astype(jnp.bfloat16)
        )
        return [
            send(left_ref.at[slot], left_ref.at[slot + 1], CORE),
            send(gate_send_ref.at[slot // 2], gate_ref.at[slot + 1], CORE),
        ]

    @pl.loop(0, rows)
    def _(row):
        project(row, 0, row)
        gates(row)

    core_copies = finish_rows(0)
    forward = []

    def pass_on(at):
        z_copies[at].wait_recv()
        part = pl.ds(at * part_size, part_size)
        forward.append(send(right_ref.at[1, part], right_ref.at[3, part], Y))

    for at in range(FAR_CHUNKS):
        if at < RIGHT_CHUNKS:
            pass_on(at)
        far_copies[at].wait_recv()

        @pl.loop(at * far_rows, (at + 1) * far_rows)
        def _(row):
            normalise(far_ref, row)
            project(row, 0, rows + row)
            gates(row)

    core_copies += finish_rows(2)
    for copy in core_copies + y_copies:
        copy.wait_recv()

    half_cols = cols // 2
    for at in range(RIGHT_CHUNKS):
        forward[at].wait_recv()

        @pl.loop(at * part_size, (at + 1) * part_size, step=4)
        def _(base):
            for more in range(4):
                chan = base + more
                right = jnp.concatenate([right_ref[slot, chan] for slot in range(4)], 0)
                left = jnp.concatenate([left_ref[slot, chan] for slot in range(4)], 0)
                tri = lax.dot_general(
                    right, left, contract_last, preferred_element_type=jnp.float32
                )
                tri = tri.astype(jnp.bfloat16).astype(jnp.float32)
                start = pl.multiple_of(chan * half_cols, half_cols)
                tri_ref[pl.ds(start, half_cols), :] = jnp.concatenate(
                    [tri[:half_cols], tri[half_cols:]], 1
                )

    def finish_col(col):
        tri = tri_ref[pl.ds(col, hidden, stride=half_cols), :]
        normed = layer_norm(tri, out_gain_ref[...], out_bias_ref[...], 0).astype(jnp.bfloat16)
        mixed = lax.dot_general(
            normed, last_w_ref[...], contract_first, preferred_element_type=jnp.float32
        )
        for upper in range(2):
            at = col + upper * half_cols
            gate = jnp.concatenate([gate_ref[slot, at] for slot in range(4)], 0)
            part = mixed[upper * cols : (upper + 1) * cols]
            update_ref[at] = (part * gate.astype(jnp.float32)).astype(jnp.bfloat16)

    blocks = (0, CORE, HALF, HALF | CORE)
    places = [
        pl.ds(pl.multiple_of(other(me, block) * rows, rows), rows) for block in blocks
    ]
    for low in (1, 0):

        @pl.loop(low * rows, (low + 1) * rows)
        def _(col):
            finish_col(col)

        for chip_at in (low + 2, low):
            for at, place in enumerate(places):
                src = update_ref.at[
                    chip_at * rows : (chip_at + 1) * rows, at * rows : (at + 1) * rows, :
                ]
                if chip_at:
                    send(src, out_ref.at[:, place, :], CHIPS[chip_at])
                else:
                    out_ref[:, place, :] = src[...]

    for copy in started:
        copy.wait_send()
    for copy in started[-12:]:
        copy.wait_recv()


def half_shards(
    pair, pad_mask, w_in, in_exps, w_out, out_exps, in_gain, in_bias, out_gain, out_bias
):
    rows, whole_len, _ = pair.shape
    hidden = w_out.shape[0]
    me = lax.axis_index("ia")
    w_eff = scaled_weight(w_in, in_exps)
    w_last = scaled_weight(w_out, out_exps)
    mask_f = pad_mask.astype(jnp.float32)
    mask_rows = jnp.concatenate(
        [
            lax.dynamic_slice_in_dim(mask_f, owner * rows, rows, 0)
            for owner in (me, other(me, HALF))
        ]
    )
    masks = mask_rows[:, None, None] * mask_f[None, None, :]
    cols = 4 * rows
    vmem = pl.BlockSpec(memory_space=pltpu.VMEM)
    copies = FAR_CHUNKS + 3 * RIGHT_CHUNKS + 4 + 12
    return pl.pallas_call(
        functools.partial(triangle, rows, whole_len, hidden),
        out_shape=jax.ShapeDtypeStruct(pair.shape, jnp.bfloat16),
        in_specs=[vmem] * 9,
        out_specs=vmem,
        scratch_shapes=[
            pltpu.VMEM(pair.shape, jnp.bfloat16),
            pltpu.VMEM(pair.shape, jnp.bfloat16),
            pltpu.VMEM((whole_len // 128, hidden * rows, 128), jnp.float32),
            pltpu.VMEM((2 * cols * rows, hidden), jnp.float32),
            pltpu.VMEM((4, hidden, rows, whole_len), jnp.bfloat16),
            pltpu.VMEM((4, hidden, rows, whole_len), jnp.bfloat16),
            pltpu.VMEM((4, cols, rows, hidden), jnp.bfloat16),
            pltpu.VMEM((2, cols, rows, hidden), jnp.bfloat16),
            pltpu.VMEM((hidden * cols // 2, 2 * cols), jnp.float32),
            pltpu.VMEM((cols, cols, hidden), jnp.bfloat16),
            pltpu.SemaphoreType.DMA((copies,)),
            pltpu.SemaphoreType.DMA((copies,)),
        ],
        compiler_params=pltpu.CompilerParams(
            collective_id=0, has_side_effects=True, vmem_limit_bytes=40 * 2**20
        ),
    )(
        pair,
        masks,
        w_eff[:, : 4 * hidden].T,
        w_eff[:, 4 * hidden :],
        w_last,
        in_gain[None, :],
        in_bias[None, :],
        out_gain[:, None],
        out_bias[:, None],
    )


def solution(mesh):
    count = mesh.shape["ia"]
    body = half_shards if count == 16 else shards
    return jax.shard_map(
        body,
        mesh=mesh,
        in_specs=(
            P(("groups", "ia"), None, None),
            P("groups"),
            P(),
            P(),
            P(),
            P(),
            P(),
            P(),
            P(),
            P(),
        ),
        out_specs=P(("groups", "ia"), None, None),
        check_vma=False,
    )
```

```python
import functools

import jax
import jax.numpy as jnp
from jax import lax
from jax.experimental import pallas as pl
from jax.experimental.pallas import tpu as pltpu
from jax.sharding import PartitionSpec as P

BLK = 32


def layer_norm(values, gain, bias, axis):
    mean_val = jnp.mean(values, axis=axis, keepdims=True)
    centred = values - mean_val
    variance = jnp.mean(centred * centred, axis=axis, keepdims=True)
    return centred * lax.rsqrt(variance + 1e-05) * gain + bias


def scaled_weight(weight, exponents):
    factor = jnp.repeat(jnp.exp2(exponents.astype(jnp.float32)), BLK)
    return (weight.astype(jnp.float32) * factor[None, :]).astype(jnp.bfloat16)


def shards(pair, pad_mask, w_in, in_exps, w_out, out_exps, in_gain, in_bias, out_gain, out_bias):
    tok_rows = pair.shape[0]
    whole_len = pair.shape[1]
    width_in = pair.shape[2]
    hidden = w_out.shape[0]
    row_start = lax.axis_index("ia") * tok_rows
    w_eff = scaled_weight(w_in, in_exps)
    w_last = scaled_weight(w_out, out_exps)
    mask_f = pad_mask.astype(jnp.float32)
    mask_rows = lax.dynamic_slice_in_dim(mask_f, row_start, tok_rows, 0)
    normed = layer_norm(pair.astype(jnp.float32), in_gain, in_bias, -1).astype(jnp.bfloat16)
    proj = jnp.dot(
        normed.reshape(tok_rows * whole_len, width_in), w_eff, preferred_element_type=jnp.float32
    )
    proj = proj.reshape(tok_rows, whole_len, 5 * hidden)
    pair_mask = mask_rows[:, None, None] * mask_f[None, :, None]
    left = (
        jax.nn.sigmoid(proj[:, :, 0:hidden]) * proj[:, :, hidden : 2 * hidden] * pair_mask
    ).astype(jnp.bfloat16)
    right = (
        jax.nn.sigmoid(proj[:, :, 2 * hidden : 3 * hidden])
        * proj[:, :, 3 * hidden : 4 * hidden]
        * pair_mask
    ).astype(jnp.bfloat16)
    gate = jax.nn.sigmoid(proj[:, :, 4 * hidden : 5 * hidden]).astype(jnp.bfloat16)
    left_t = jnp.transpose(left, (2, 0, 1))
    right_t = jnp.transpose(right, (2, 0, 1))
    left_chan, right_chan = (
        lax.all_to_all(left_t, "ia", split_axis=0, concat_axis=1, tiled=True),
        lax.all_to_all(right_t, "ia", split_axis=0, concat_axis=1, tiled=True),
    )
    gate_moved = lax.all_to_all(gate, "ia", split_axis=1, concat_axis=0, tiled=True)
    gate_cols = jnp.swapaxes(gate_moved, 0, 1)
    tri_t = jnp.einsum(
        "hjk,hik->hji", right_chan, left_chan, preferred_element_type=jnp.float32
    ).astype(jnp.bfloat16)
    tri_cols = lax.all_to_all(tri_t, "ia", split_axis=1, concat_axis=0, tiled=True)
    tri_norm = layer_norm(
        tri_cols.astype(jnp.float32), out_gain[:, None, None], out_bias[:, None, None], 0
    ).astype(jnp.bfloat16)
    mixed = jnp.einsum("hji,hc->jic", tri_norm, w_last, preferred_element_type=jnp.float32)
    return (mixed * gate_cols.astype(jnp.float32)).astype(jnp.bfloat16)


CORE, Y, Z, HALF = 1, 2, 4, 8
CHIPS = (0, Z, Y, Z | Y)
FAR_CHUNKS = 4
RIGHT_CHUNKS = 4


def other(me, bits):
    for bit in (CORE, Y, Z, HALF):
        if bits & bit:
            me = me + bit * (1 - 2 * ((me // bit) % 2))
    return me


def sigmoid(values):
    return 0.5 + 0.5 * jnp.tanh(0.5 * values)


def triangle(
    rows,
    whole_len,
    hidden,
    pair_ref,
    mask_ref,
    side_w_ref,
    gate_w_ref,
    last_w_ref,
    in_gain_ref,
    in_bias_ref,
    out_gain_ref,
    out_bias_ref,
    out_ref,
    far_ref,
    norm_ref,
    stage_ref,
    gate_stage_ref,
    right_ref,
    left_ref,
    gate_ref,
    gate_send_ref,
    tri_ref,
    update_ref,
    send_sem,
    recv_sem,
):
    me = lax.axis_index("ia")
    barrier = pltpu.get_barrier_semaphore()
    peers = (CORE, Y, Z, Z | Y, HALF)
    for bits in peers:
        pl.semaphore_signal(
            barrier, inc=1, device_id={"ia": other(me, bits)}, device_id_type=pl.DeviceIdType.MESH
        )
    pl.semaphore_wait(barrier, len(peers))

    started = []

    def send(src, dst, bits):
        at = len(started)
        copy = pltpu.make_async_remote_copy(
            src_ref=src,
            dst_ref=dst,
            send_sem=send_sem.at[at],
            recv_sem=recv_sem.at[at],
            device_id={"ia": other(me, bits)},
            device_id_type=pl.DeviceIdType.MESH,
        )
        copy.start()
        started.append(copy)
        return copy

    far_rows = rows // FAR_CHUNKS
    far_copies = []
    for at in range(FAR_CHUNKS):
        part = pl.ds(at * far_rows, far_rows)
        far_copies.append(send(pair_ref.at[part], far_ref.at[part], HALF))

    contract_last = (((1,), (1,)), ((), ()))
    contract_first = (((0,), (0,)), ((), ()))

    def normalise(src_ref, row):
        values = src_ref[row].astype(jnp.float32)
        normed = layer_norm(values, in_gain_ref[...], in_bias_ref[...], -1)
        norm_ref[row] = normed.astype(jnp.bfloat16)

    def project(row, side, mask_row):
        weight = side_w_ref[side * 2 * hidden : (side + 1) * 2 * hidden, :]
        proj = lax.dot_general(
            weight, norm_ref[row], contract_last, preferred_element_type=jnp.float32
        )
        value = sigmoid(proj[:hidden]) * proj[hidden:] * mask_ref[mask_row]
        for lane in range(whole_len // 128):
            stage_ref[lane, pl.ds(row, hidden, stride=rows), :] = value[
                :, lane * 128 : (lane + 1) * 128
            ]

    def unstage(dst_ref, slot, start, size):
        for lane in range(whole_len // 128):
            dst_ref[slot, start : start + size, :, lane * 128 : (lane + 1) * 128] = (
                stage_ref[lane, start * rows : (start + size) * rows, :]
                .reshape(size, rows, 128)
                .astype(jnp.bfloat16)
            )

    @pl.loop(0, rows, unroll=4)
    def _(row):
        normalise(pair_ref, row)
        project(row, 1, row)

    part_size = hidden // RIGHT_CHUNKS
    z_copies, y_copies = [], []
    for at in range(RIGHT_CHUNKS):
        unstage(right_ref, 0, at * part_size, part_size)
        part = pl.ds(at * part_size, part_size)
        z_copies.append(send(right_ref.at[0, part], right_ref.at[1, part], Z))
        y_copies.append(send(right_ref.at[0, part], right_ref.at[2, part], Y))

    gate_cols = [
        pl.ds(pl.multiple_of(other(me, core | chip) * rows, rows), rows)
        for core in (0, CORE)
        for chip in CHIPS
    ]
    cols = rows * len(CHIPS)

    def gates(row):
        picked = jnp.concatenate([norm_ref[row, part, :] for part in gate_cols], 0)
        gate = sigmoid(jnp.dot(picked, gate_w_ref[...], preferred_element_type=jnp.float32))
        gate_stage_ref[pl.ds(row, 2 * cols, stride=rows), :] = gate

    def finish_rows(slot):
        unstage(left_ref, slot, 0, hidden)
        gate_ref[slot] = (
            gate_stage_ref[0 : cols * rows, :].reshape(cols, rows, hidden).astype(jnp.bfloat16)
        )
        gate_send_ref[slot // 2] = (
            gate_stage_ref[cols * rows :, :].reshape(cols, rows, hidden).astype(jnp.bfloat16)
        )
        return [
            send(left_ref.at[slot], left_ref.at[slot + 1], CORE),
            send(gate_send_ref.at[slot // 2], gate_ref.at[slot + 1], CORE),
        ]

    @pl.loop(0, rows, unroll=4)
    def _(row):
        project(row, 0, row)
        gates(row)

    core_copies = finish_rows(0)
    forward = []

    def pass_on(at):
        z_copies[at].wait_recv()
        part = pl.ds(at * part_size, part_size)
        forward.append(send(right_ref.at[1, part], right_ref.at[3, part], Y))

    for at in range(FAR_CHUNKS):
        if at < RIGHT_CHUNKS:
            pass_on(at)
        far_copies[at].wait_recv()

        @pl.loop(at * far_rows, (at + 1) * far_rows, unroll=4)
        def _(row):
            normalise(far_ref, row)
            project(row, 0, rows + row)
            gates(row)

    core_copies += finish_rows(2)
    for copy in core_copies + y_copies:
        copy.wait_recv()

    half_cols = cols // 2
    gain_col, bias_col = (
        jnp.broadcast_to(ref[...], (2 * cols, hidden)).T for ref in (out_gain_ref, out_bias_ref)
    )
    for at in range(RIGHT_CHUNKS):
        forward[at].wait_recv()

        @pl.loop(at * part_size, (at + 1) * part_size, step=4)
        def _(base):
            for more in range(4):
                chan = base + more
                right = jnp.concatenate([right_ref[slot, chan] for slot in range(4)], 0)
                left = jnp.concatenate([left_ref[slot, chan] for slot in range(4)], 0)
                tri = lax.dot_general(
                    right, left, contract_last, preferred_element_type=jnp.float32
                )
                tri = tri.astype(jnp.bfloat16).astype(jnp.float32)
                start = pl.multiple_of(chan * half_cols, half_cols)
                tri_ref[pl.ds(start, half_cols), :] = jnp.concatenate(
                    [tri[:half_cols], tri[half_cols:]], 1
                )

    def finish_col(col):
        tri = tri_ref[pl.ds(col, hidden, stride=half_cols), :]
        normed = layer_norm(tri, gain_col, bias_col, 0).astype(jnp.bfloat16)
        mixed = lax.dot_general(
            normed, last_w_ref[...], contract_first, preferred_element_type=jnp.float32
        )
        for upper in range(2):
            at = col + upper * half_cols
            gate = jnp.concatenate([gate_ref[slot, at] for slot in range(4)], 0)
            part = mixed[upper * cols : (upper + 1) * cols]
            update_ref[at] = (part * gate.astype(jnp.float32)).astype(jnp.bfloat16)

    blocks = (0, CORE, HALF, HALF | CORE)
    places = [
        pl.ds(pl.multiple_of(other(me, block) * rows, rows), rows) for block in blocks
    ]
    for low in (1, 0):

        @pl.loop(low * rows, (low + 1) * rows, unroll=4)
        def _(col):
            finish_col(col)

        for chip_at in (low + 2, low):
            for at, place in enumerate(places):
                src = update_ref.at[
                    chip_at * rows : (chip_at + 1) * rows, at * rows : (at + 1) * rows, :
                ]
                if chip_at:
                    send(src, out_ref.at[:, place, :], CHIPS[chip_at])
                else:
                    out_ref[:, place, :] = src[...]

    for copy in started:
        copy.wait_send()
    for copy in started[-12:]:
        copy.wait_recv()


def half_shards(
    pair, pad_mask, w_in, in_exps, w_out, out_exps, in_gain, in_bias, out_gain, out_bias
):
    rows, whole_len, _ = pair.shape
    hidden = w_out.shape[0]
    me = lax.axis_index("ia")
    w_eff = scaled_weight(w_in, in_exps)
    w_last = scaled_weight(w_out, out_exps)
    mask_f = pad_mask.astype(jnp.float32)
    mask_rows = jnp.concatenate(
        [
            lax.dynamic_slice_in_dim(mask_f, owner * rows, rows, 0)
            for owner in (me, other(me, HALF))
        ]
    )
    masks = mask_rows[:, None, None] * mask_f[None, None, :]
    cols = 4 * rows
    vmem = pl.BlockSpec(memory_space=pltpu.VMEM)
    copies = FAR_CHUNKS + 3 * RIGHT_CHUNKS + 4 + 12
    return pl.pallas_call(
        functools.partial(triangle, rows, whole_len, hidden),
        out_shape=jax.ShapeDtypeStruct(pair.shape, jnp.bfloat16),
        in_specs=[vmem] * 9,
        out_specs=vmem,
        scratch_shapes=[
            pltpu.VMEM(pair.shape, jnp.bfloat16),
            pltpu.VMEM(pair.shape, jnp.bfloat16),
            pltpu.VMEM((whole_len // 128, hidden * rows, 128), jnp.float32),
            pltpu.VMEM((2 * cols * rows, hidden), jnp.float32),
            pltpu.VMEM((4, hidden, rows, whole_len), jnp.bfloat16),
            pltpu.VMEM((4, hidden, rows, whole_len), jnp.bfloat16),
            pltpu.VMEM((4, cols, rows, hidden), jnp.bfloat16),
            pltpu.VMEM((2, cols, rows, hidden), jnp.bfloat16),
            pltpu.VMEM((hidden * cols // 2, 2 * cols), jnp.float32),
            pltpu.VMEM((cols, cols, hidden), jnp.bfloat16),
            pltpu.SemaphoreType.DMA((copies,)),
            pltpu.SemaphoreType.DMA((copies,)),
        ],
        compiler_params=pltpu.CompilerParams(
            collective_id=0, has_side_effects=True, vmem_limit_bytes=40 * 2**20
        ),
    )(
        pair,
        masks,
        w_eff[:, : 4 * hidden].T,
        w_eff[:, 4 * hidden :],
        w_last,
        in_gain[None, :],
        in_bias[None, :],
        out_gain[None, :],
        out_bias[None, :],
    )


def solution(mesh):
    count = mesh.shape["ia"]
    body = half_shards if count == 16 else shards
    return jax.shard_map(
        body,
        mesh=mesh,
        in_specs=(
            P(("groups", "ia"), None, None),
            P("groups"),
            P(),
            P(),
            P(),
            P(),
            P(),
            P(),
            P(),
            P(),
        ),
        out_specs=P(("groups", "ia"), None, None),
        check_vma=False,
    )
```
